256 devices in a mesh: src: 32 (over z, y), rcv: 8 (over x, core).
Axes of the slice: x: 4, y: 4, z: 8, core: 2. Of those that a mesh axis runs over, the one named last changes fastest.
Arguments:
- src_traces: bfloat16 [2, 8, 1024, 2048], P(None, 'rcv', 'src'), may hold values from -6 to 6
- rcv_traces: bfloat16 [2, 32, 1024, 2048], P(None, 'src', 'rcv'), may hold values from -6 to 6
- src_owner: int32 [2, 32], P(None, 'src'), may hold values from 0 to 7
- rcv_owner: int32 [2, 8], P(None, 'rcv'), may hold values from 0 to 31
- active: int32 [32, 32], P('src', 'rcv'), may hold values 0 or 1
Outputs:
- stacked: float32 [1024, 1024, 128], P('src', 'rcv')
The draws below stay inside these ranges and needn't reach their ends.
Inputs may be any that keep to these rules, and one draw needn't show every extreme that they name: src_owner names a slot of the rcv dimension. rcv_owner names a slot of the src dimension.
All inputs are finite; a program needn't handle non-finite values. No bound on the sum of `active` on one device may be relied on, other than what follows from the above.
Results may differ from the reference program's by a relative error of at most 0.004.
Values may be sent and summed in bfloat16 or wider, within the bound.
A program may use at most 128 MiB of HBM per device.

```python
import jax
import jax.numpy as jnp
from jax import lax

SRC_DEV = 32
RCV_DEV = 128
SAMPLES = 2048
LAGS = 128
BLOCK = 32
WINDOWS = 2
SOURCES = 1024
RECEIVERS = 1024
N_SRC = 32
N_RCV = 8


def plant(array, key, smallest, high):
    dims = array.shape
    place = [jax.random.randint(jax.random.fold_in(key, axis), (), 0, dims[axis]) for axis in range(len(dims))]
    array = array.at[tuple(place)].set(smallest)
    longest = dims.index(max(dims))
    place[longest] = (place[longest] + 1) % dims[longest]
    return array.at[tuple(place)].set(high)


def steps_of(stream_key, shape, split, low, largest):
    gain, own = 1.0, jax.random.fold_in(stream_key, 6)
    for dim, parts in split:
        draws = jnp.exp(jax.random.uniform(jax.random.fold_in(own, dim), (parts,), jnp.float32, low / len(split), largest / len(split)))
        gain = gain * jnp.repeat(draws, shape[dim] // parts).reshape([-1 if axis == dim else 1 for axis in range(len(shape))])
    return gain


def noise(key, extent, width, most, shards=(), kind=jnp.bfloat16):
    result = jax.random.normal(key, extent, jnp.float32) * width
    if len(shards) > 0:
        result = steps_of(key, extent, shards, -0.22, 0.18) * result
    return jnp.clip(result, min=-most, max=most).astype(kind)


def setup_inputs(seed: int = 0) -> dict:
    streams_of = jax.random.split(jax.random.key(seed), 6)
    src_traces = noise(streams_of[0], (WINDOWS, N_RCV, SOURCES, SAMPLES), 1.0, 6.0, ((1, 8), (2, 32)))
    rcv_traces = noise(streams_of[1], (WINDOWS, N_SRC, RECEIVERS, SAMPLES), 1.0, 6.0, ((1, 32), (2, 8)))
    src_owner = plant(jax.random.randint(streams_of[2], (WINDOWS, N_SRC), 0, N_RCV), jax.random.fold_in(streams_of[2], 1), 0, N_RCV - 1).astype(jnp.int32)
    rcv_owner = plant(jax.random.randint(streams_of[3], (WINDOWS, N_RCV), 0, N_SRC), jax.random.fold_in(streams_of[3], 1), 0, N_SRC - 1).astype(jnp.int32)
    active = plant((jax.random.randint(streams_of[4], (SOURCES // BLOCK, RECEIVERS // BLOCK), 0, 2) < 1).astype(jnp.int32), jax.random.fold_in(streams_of[4], 1), 0, 1)
    return {"src_traces": src_traces, "rcv_traces": rcv_traces, "src_owner": src_owner, "rcv_owner": rcv_owner, "active": active}


epsilon = 1e-06

def normalise(traces):
    values = traces.astype(jnp.float32)
    energy = lax.optimization_barrier(jnp.mean(values * values, axis=-1, keepdims=True))
    return (values * lax.rsqrt(energy + epsilon)).astype(jnp.bfloat16)

def reference(src_traces, rcv_traces, src_owner, rcv_owner, active):
    src_chan = jnp.arange(SOURCES, dtype=jnp.int32)
    rcv_chan = jnp.arange(RECEIVERS, dtype=jnp.int32)
    src_group = src_chan // SRC_DEV
    rcv_group = rcv_chan // RCV_DEV
    span = SAMPLES - LAGS
    totals = jnp.zeros((SOURCES, RECEIVERS, LAGS), jnp.float32)
    for window in range(WINDOWS):
        first = normalise(src_traces[window, src_owner[window][src_group], src_chan]).astype(jnp.float32)
        second = normalise(rcv_traces[window, rcv_owner[window][rcv_group], rcv_chan]).astype(jnp.float32)
        leading = first[:, :span]

        def one_lag(shift):
            moved = lax.dynamic_slice_in_dim(second, shift, span, 1)
            return jnp.dot(leading, moved.T, precision=lax.Precision.HIGHEST, preferred_element_type=jnp.float32)
        per_lag = lax.map(one_lag, jnp.arange(LAGS, dtype=jnp.int32))
        totals = totals + jnp.transpose(per_lag, (1, 2, 0))
    listed = jnp.repeat(jnp.repeat(active, BLOCK, axis=0), BLOCK, axis=1).astype(jnp.float32)
    scale = 1.0 / jnp.sqrt(jnp.float32(span * WINDOWS))
    return totals * listed[:, :, None] * scale
```

```python
import jax
import jax.numpy as jnp
from jax import lax
from jax.experimental import pallas as pl
from jax.experimental.pallas import tpu as pltpu
from jax.sharding import PartitionSpec as P

LAGS = 128
BLOCK = 32
FINE = 16

epsilon = 1e-06


def from_root(value, axis, source):
    kept = jnp.where(lax.axis_index(axis) == source, value, 0).astype(value.dtype)
    return lax.psum(kept, axis)


def normalise(traces):
    values = traces.astype(jnp.float32)
    energy = jnp.mean(values * values, axis=-1, keepdims=True)
    return (values * lax.rsqrt(energy + epsilon)).astype(jnp.bfloat16)


def correlate_kernel(active_ref, a_ref, bt_ref, out_hbm, toep, lagged, out_v, sem):
    wins, src, samples = a_ref.shape
    scale = 1.0 / (float((samples - LAGS) * wins) ** 0.5)
    lane = lax.broadcasted_iota(jnp.int32, (src, samples), 1)
    for w in range(wins):
        a = jnp.where(lane < samples - LAGS, a_ref[w].astype(jnp.float32), 0.0)
        for k in range(FINE):
            rolled = a if k == 0 else pltpu.roll(a, k, 1)
            toep[k * src : (k + 1) * src, w * samples : (w + 1) * samples] = rolled.astype(jnp.bfloat16)
    depth = wins * samples
    group = lax.broadcasted_iota(jnp.int32, (1, LAGS), 1) // BLOCK
    factor = jnp.zeros((1, LAGS), jnp.float32)
    for g in range(LAGS // BLOCK):
        factor = jnp.where(group == g, active_ref[0, g].astype(jnp.float32) * scale, factor)

    def step(pair, carry):
        base = pl.multiple_of(pair * 2 * FINE, FINE)
        both = jnp.concatenate([bt_ref[pl.ds(base, depth), :], bt_ref[pl.ds(base + FINE, depth), :]], axis=1)
        acc = jnp.dot(toep[...], both, preferred_element_type=jnp.float32)
        for jj in range(2):
            for k in range(FINE):
                lagged[pl.ds(base + FINE * jj + k, src, stride=LAGS), :] = (
                    acc[k * src : (k + 1) * src, jj * 128 : (jj + 1) * 128] * factor
                )
        return carry

    lax.fori_loop(0, LAGS // FINE // 2, step, 0)
    for s in range(src):
        out_v[s] = lagged[s * LAGS : (s + 1) * LAGS, :].T
        if s % 8 == 7:
            part = pl.ds(s - 7, 8)
            pltpu.make_async_copy(out_v.at[part], out_hbm.at[part], sem.at[s // 8]).start()
    for q in range(src // 8):
        part = pl.ds(q * 8, 8)
        pltpu.make_async_copy(out_v.at[part], out_hbm.at[part], sem.at[q]).wait()


def correlate(active, a, bt):
    wins, src, samples = a.shape
    rcv = bt.shape[1]
    return pl.pallas_call(
        correlate_kernel,
        out_shape=jax.ShapeDtypeStruct((src, rcv, LAGS), jnp.float32),
        in_specs=[
            pl.BlockSpec(memory_space=pltpu.SMEM),
            pl.BlockSpec(memory_space=pltpu.VMEM),
            pl.BlockSpec(memory_space=pltpu.VMEM),
        ],
        out_specs=pl.BlockSpec(memory_space=pl.ANY),
        scratch_shapes=[
            pltpu.VMEM((FINE * src, wins * samples), jnp.bfloat16),
            pltpu.VMEM((src * LAGS, rcv), jnp.float32),
            pltpu.VMEM((src, rcv, LAGS), jnp.float32),
            pltpu.SemaphoreType.DMA((src // 8,)),
        ],
        compiler_params=pltpu.CompilerParams(vmem_limit_bytes=48 * 2**20),
    )(active, a, bt)


def body(src_traces, rcv_traces, src_owner, rcv_owner, active):
    sources = normalise(src_traces[:, 0])
    receivers = normalise(rcv_traces[:, 0])
    wins, rcv, samples = receivers.shape
    source_rows = from_root(sources, "rcv", src_owner[:, :, None])
    receiver_rows = from_root(receivers, "src", rcv_owner[:, :, None])
    late = jnp.transpose(receiver_rows, (0, 2, 1)).reshape(wins * samples, rcv)
    late = jnp.concatenate([late, jnp.zeros((LAGS, rcv), jnp.bfloat16)], axis=0)
    return correlate(active, source_rows, late)


def solution(mesh):
    return jax.shard_map(
        body,
        mesh=mesh,
        in_specs=(
            P(None, "rcv", "src", None),
            P(None, "src", "rcv", None),
            P(None, "src"),
            P(None, "rcv"),
            P("src", "rcv"),
        ),
        out_specs=P("src", "rcv", None),
        check_vma=False,
    )
```

```python
import jax
import jax.numpy as jnp
import numpy as np
from jax import lax
from jax.experimental import pallas as pl
from jax.experimental.pallas import tpu as pltpu
from jax.sharding import PartitionSpec as P

MESH = pl.DeviceIdType.MESH
LAGS = 128
BLOCK = 32
FINE = 16
DEPTH_Z, DEPTH_Y = 8, 4

HOPS = ((0, 1), (0, 1), (1, 1), (2, 0), (0, -1), (0, -1), (-1, -1), (-2, 0))
STREAMS = len(HOPS)
CHUNKS = 8
STEPS = 4
SLACK = 5
ROUNDS = CHUNKS + (STEPS - 1) * SLACK
ROUTES = (
    (0, 0, 0, 0, 0, 0, 0, 0, 0, 0, 0, 0, 0, 0, 0, 0, 0, 0, 0, 0, 0, 0, 0, 0),
    (0, 1, 0, 1, 0, 0, 1, 0, 0, 1, 2, 6, 7, 3, 5, 4, 1, 1, 4, 4, 4, 4, 4, 4),
    (6, 1, 0, 1, 2, 3, 0, 1, 0, 1, 7, 6, 4, 5, 3, 2, 2, 2, 3, 3, 2, 2, 3, 3),
    (0, 0, 4, 5, 4, 5, 5, 4, 7, 1, 6, 0, 4, 5, 2, 3, 4, 3, 3, 4, 1, 1, 3, 3),
    (2, 0, 2, 2, 2, 3, 4, 0, 1, 3, 4, 6, 2, 7, 0, 5, 4, 3, 2, 3, 2, 4, 3, 4),
    (3, 2, 2, 2, 2, 3, 0, 2, 4, 6, 2, 7, 0, 5, 1, 3, 3, 4, 1, 3, 3, 4, 4, 3),
    (6, 1, 2, 2, 2, 6, 5, 2, 2, 7, 1, 5, 4, 6, 3, 0, 2, 4, 2, 3, 4, 3, 3, 4),
    (3, 2, 3, 2, 4, 6, 6, 6, 2, 5, 1, 6, 4, 0, 3, 7, 3, 4, 3, 2, 3, 4, 2, 4),
    (2, 3, 3, 3, 2, 7, 3, 0, 1, 4, 6, 3, 5, 0, 2, 7, 4, 3, 3, 1, 4, 3, 3, 3),
    (2, 1, 3, 3, 3, 2, 1, 2, 6, 3, 4, 1, 2, 5, 0, 7, 4, 2, 3, 2, 3, 4, 4, 4),
    (1, 3, 2, 2, 2, 5, 3, 2, 4, 3, 2, 1, 0, 5, 7, 6, 4, 3, 2, 3, 4, 3, 4, 4),
    (3, 2, 3, 3, 2, 3, 3, 2, 2, 1, 6, 0, 7, 3, 4, 5, 3, 4, 4, 4, 4, 2, 4, 4),
    (3, 2, 3, 3, 2, 3, 4, 2, 6, 7, 4, 5, 3, 2, 0, 1, 4, 4, 3, 3, 3, 3, 4, 4),
    (3, 2, 2, 3, 3, 2, 3, 2, 5, 4, 3, 2, 0, 1, 7, 6, 4, 4, 2, 2, 4, 4, 4, 4),
    (1, 2, 3, 3, 2, 3, 3, 2, 3, 2, 0, 1, 7, 6, 5, 4, 3, 3, 3, 3, 4, 4, 4, 4),
    (7, 6, 7, 2, 6, 7, 6, 6, 3, 1, 2, 0, 5, 4, 7, 6, 4, 4, 3, 4, 4, 4, 3, 3),
    (3, 7, 3, 3, 7, 3, 7, 7, 4, 5, 6, 3, 1, 0, 2, 7, 4, 4, 4, 2, 4, 4, 4, 2),
    (3, 7, 3, 0, 7, 3, 7, 1, 7, 3, 5, 0, 2, 6, 4, 1, 3, 3, 4, 3, 4, 4, 4, 3),
    (3, 7, 2, 3, 7, 3, 6, 7, 1, 0, 3, 2, 5, 4, 7, 6, 4, 4, 3, 3, 4, 4, 3, 3),
    (3, 7, 3, 5, 3, 7, 3, 7, 2, 6, 0, 5, 7, 3, 1, 4, 4, 4, 4, 3, 3, 3, 4, 3),
    (0, 7, 7, 6, 7, 6, 7, 7, 6, 7, 4, 5, 3, 2, 1, 0, 3, 3, 4, 4, 4, 4, 3, 3),
    (2, 3, 2, 2, 3, 2, 3, 6, 7, 1, 3, 2, 5, 4, 6, 0, 4, 4, 3, 3, 4, 4, 3, 4),
    (6, 7, 7, 6, 7, 6, 7, 6, 3, 2, 1, 0, 6, 7, 4, 5, 4, 4, 4, 4, 3, 3, 3, 3),
    (6, 7, 7, 6, 7, 6, 6, 7, 5, 4, 3, 2, 0, 1, 7, 6, 4, 4, 4, 4, 4, 4, 2, 2),
    (7, 6, 7, 0, 7, 6, 7, 7, 4, 0, 6, 3, 1, 5, 2, 7, 3, 4, 3, 3, 3, 4, 3, 1),
    (6, 7, 0, 6, 7, 6, 7, 7, 7, 2, 1, 3, 5, 6, 4, 0, 2, 4, 4, 4, 4, 3, 3, 2),
    (6, 1, 4, 6, 6, 4, 6, 6, 1, 7, 3, 2, 4, 0, 6, 5, 3, 3, 4, 4, 3, 4, 2, 3),
    (6, 7, 7, 4, 7, 4, 7, 7, 1, 6, 5, 3, 7, 2, 0, 4, 4, 3, 4, 4, 2, 4, 3, 2),
    (2, 6, 5, 6, 5, 6, 6, 6, 3, 6, 5, 1, 2, 0, 7, 4, 4, 2, 3, 4, 3, 4, 4, 3),
    (1, 7, 2, 2, 2, 7, 7, 6, 6, 1, 7, 3, 0, 5, 4, 2, 3, 3, 2, 4, 4, 3, 3, 2),
    (6, 7, 4, 4, 4, 6, 6, 6, 7, 0, 1, 5, 3, 6, 4, 2, 3, 4, 3, 4, 4, 2, 2, 3),
    (0, 7, 0, 6, 6, 7, 6, 6, 1, 5, 4, 7, 2, 0, 6, 3, 4, 3, 4, 3, 4, 3, 1, 3),
)

epsilon = 1e-06


def normalised(values):
    energy = jnp.mean(values * values, axis=-1, keepdims=True)
    return values * lax.rsqrt(energy + epsilon)


def spread_kernel(routes, src_owner, rcv_owner, src_ref, rcv_ref, a_out, bt_out, a_own, a_cand, a_all, own, *rest):
    wins = rcv_ref.shape[0]
    samples = rcv_ref.shape[-1]
    held = [rest[w * ROUNDS : (w + 1) * ROUNDS] for w in range(wins)]
    sent = [rest[(wins + w) * ROUNDS : (wins + w + 1) * ROUNDS] for w in range(wins)]
    send_sem, recv_sem, a_send, a_recv = rest[2 * wins * ROUNDS :]
    place = lax.axis_index("src")
    me = lax.axis_index("rcv")
    z, y = place // DEPTH_Y, place % DEPTH_Y
    others = a_own.shape[0] - 1

    def partner(i):
        dz, dy = HOPS[i]
        return {"src": lax.rem(z + dz + DEPTH_Z, DEPTH_Z) * DEPTH_Y + lax.rem(y + dy + DEPTH_Y, DEPTH_Y)}

    def peer(i):
        return lax.rem(me + 1 + i, others + 1)

    barrier = pltpu.get_barrier_semaphore()
    seen = []
    for i in range(STREAMS):
        if HOPS[i] not in seen:
            seen.append(HOPS[i])
            pl.semaphore_signal(barrier, inc=1, device_id=partner(i), device_id_type=MESH)
    for i in range(others):
        pl.semaphore_signal(barrier, inc=1, device_id={"rcv": peer(i)}, device_id_type=MESH)

    width = samples // (others + 1)
    for w in range(wins):
        rows = normalised(src_ref[w, 0].astype(jnp.float32)).astype(jnp.bfloat16)
        for i in range(others + 1):
            a_own[i, w] = rows[:, i * width : (i + 1) * width]
        rows = normalised(rcv_ref[w, 0].astype(jnp.float32))
        for t in range(samples // LAGS):
            own[pl.ds(w * samples + t * LAGS, LAGS), :] = rows[:, t * LAGS : (t + 1) * LAGS].T.astype(jnp.bfloat16)
    pl.semaphore_wait(barrier, len(seen) + others)

    piece = samples // (CHUNKS * STREAMS)

    def rows_of(w, c, j):
        return pl.ds(w * samples + (c * STREAMS + j) * piece, piece)

    root, row = [], []
    for w in range(wins):
        far = rcv_owner[w, 0]
        root.append(far == place)
        dz = lax.rem(z - far // DEPTH_Y + DEPTH_Z, DEPTH_Z)
        dy = lax.rem(y - far % DEPTH_Y + DEPTH_Y, DEPTH_Y)
        row.append((dz * DEPTH_Y + dy) * (3 * STREAMS))

    def arrived(w, r):
        pltpu.make_async_copy(held[w][r], held[w][r], recv_sem.at[w, r]).wait()

    def a_wait(sem, k, ref):
        pltpu.make_async_copy(ref.at[pl.ds(0, others)], ref.at[pl.ds(0, others)], sem.at[k]).wait()

    for i in range(others):
        pltpu.make_async_remote_copy(
            src_ref=a_own.at[peer(i)],
            dst_ref=a_cand.at[me],
            send_sem=a_send.at[0],
            recv_sem=a_recv.at[0],
            device_id={"rcv": peer(i)},
            device_id_type=MESH,
        ).start()

    def a_pass():
        a_wait(a_recv, 0, a_cand)
        for w in range(wins):
            who = src_owner[w, 0]
            a_all[me, w] = jnp.where(who == me, a_own[me, w], a_cand[who, w])
        for i in range(others):
            pltpu.make_async_remote_copy(
                src_ref=a_all.at[me],
                dst_ref=a_all.at[me],
                send_sem=a_send.at[1],
                recv_sem=a_recv.at[1],
                device_id={"rcv": peer(i)},
                device_id_type=MESH,
            ).start()

    forward = [[routes[row[w] + i] for i in range(STREAMS)] for w in range(wins)]
    for r in range(ROUNDS):
        for w in range(wins):
            if r >= SLACK:
                arrived(w, r - SLACK)
                for i in range(STREAMS):
                    value = held[w][r - SLACK][forward[w][i]]
                    if r < CHUNKS:
                        value = jnp.where(root[w], own[rows_of(w, r, i), :], value)
                    sent[w][r][i] = value
            for i in range(STREAMS):
                pltpu.make_async_remote_copy(
                    src_ref=sent[w][r].at[i] if r >= SLACK else own.at[rows_of(w, min(r, CHUNKS - 1), i), :],
                    dst_ref=held[w][r].at[i],
                    send_sem=send_sem.at[w, r],
                    recv_sem=recv_sem.at[w, r],
                    device_id=partner(i),
                    device_id_type=MESH,
                ).start()
        if r == SLACK:
            a_pass()
    for r in range(max(0, ROUNDS - SLACK), ROUNDS):
        for w in range(wins):
            arrived(w, r)

    for w in range(wins):
        slot = [routes[row[w] + STREAMS + j] for j in range(STREAMS)]
        step = [routes[row[w] + 2 * STREAMS + j] for j in range(STREAMS)]
        for c in range(CHUNKS):
            for j in range(STREAMS):
                value = own[rows_of(w, c, j), :]
                for d in range(1, STEPS + 1):
                    value = jnp.where(step[j] == d, held[w][c + (d - 1) * SLACK][slot[j]], value)
                bt_out[rows_of(w, c, j), :] = value
    bt_out[pl.ds(wins * samples, LAGS), :] = jnp.zeros((LAGS, bt_out.shape[1]), jnp.bfloat16)
    a_wait(a_recv, 1, a_all)
    a_out[...] = a_all[...]

    a_wait(a_send, 0, a_all)
    a_wait(a_send, 1, a_all)
    for r in range(ROUNDS):
        for w in range(wins):
            pltpu.make_async_copy(held[w][r], held[w][r], send_sem.at[w, r]).wait()


def spread(src_owner, rcv_owner, src_traces, rcv_traces, peers):
    wins, _, src, samples = src_traces.shape
    rcv = rcv_traces.shape[2]
    routes = jnp.asarray(np.array(ROUTES, np.int32).reshape(-1))
    piece = samples // (CHUNKS * STREAMS)
    parts = pltpu.VMEM((peers, wins, src, samples // peers), jnp.bfloat16)
    smem, vmem = pl.BlockSpec(memory_space=pltpu.SMEM), pl.BlockSpec(memory_space=pltpu.VMEM)
    return pl.pallas_call(
        spread_kernel,
        out_shape=(
            jax.ShapeDtypeStruct((peers, wins, src, samples // peers), jnp.bfloat16),
            jax.ShapeDtypeStruct((wins * samples + LAGS, rcv), jnp.bfloat16),
        ),
        in_specs=[smem, smem, smem, vmem, vmem],
        out_specs=(vmem, vmem),
        scratch_shapes=[parts, parts, parts, pltpu.VMEM((wins * samples, rcv), jnp.bfloat16)]
        + [pltpu.VMEM((STREAMS, piece, rcv), jnp.bfloat16)] * (2 * wins * ROUNDS)
        + [
            pltpu.SemaphoreType.DMA((wins, ROUNDS)),
            pltpu.SemaphoreType.DMA((wins, ROUNDS)),
            pltpu.SemaphoreType.DMA((2,)),
            pltpu.SemaphoreType.DMA((2,)),
        ],
        compiler_params=pltpu.CompilerParams(collective_id=0, has_side_effects=True, vmem_limit_bytes=40 * 2**20),
    )(routes, src_owner, rcv_owner, src_traces, rcv_traces)


def correlate_kernel(active_ref, a_ref, bt_ref, out_hbm, toep, lagged, out_v, sem):
    parts, wins, src, width = a_ref.shape
    samples = parts * width
    scale = 1.0 / (float((samples - LAGS) * wins) ** 0.5)
    lane = lax.broadcasted_iota(jnp.int32, (src, samples), 1)
    for w in range(wins):
        a = jnp.concatenate([a_ref[i, w] for i in range(parts)], axis=1).astype(jnp.float32)
        a = jnp.where(lane < samples - LAGS, a, 0.0)
        for k in range(FINE):
            rolled = a if k == 0 else pltpu.roll(a, k, 1)
            toep[k * src : (k + 1) * src, w * samples : (w + 1) * samples] = rolled.astype(jnp.bfloat16)
    depth = wins * samples
    group = lax.broadcasted_iota(jnp.int32, (1, LAGS), 1) // BLOCK
    factor = jnp.zeros((1, LAGS), jnp.float32)
    for g in range(LAGS // BLOCK):
        factor = jnp.where(group == g, active_ref[0, g].astype(jnp.float32) * scale, factor)

    def step(pair, carry):
        base = pl.multiple_of(pair * 2 * FINE, FINE)
        both = jnp.concatenate([bt_ref[pl.ds(base, depth), :], bt_ref[pl.ds(base + FINE, depth), :]], axis=1)
        acc = jnp.dot(toep[...], both, preferred_element_type=jnp.float32)
        for jj in range(2):
            for k in range(FINE):
                lagged[pl.ds(base + FINE * jj + k, src, stride=LAGS), :] = (
                    acc[k * src : (k + 1) * src, jj * 128 : (jj + 1) * 128] * factor
                )
        return carry

    lax.fori_loop(0, LAGS // FINE // 2, step, 0)
    for s in range(src):
        out_v[s] = lagged[s * LAGS : (s + 1) * LAGS, :].T
        if s % 8 == 7:
            part = pl.ds(s - 7, 8)
            pltpu.make_async_copy(out_v.at[part], out_hbm.at[part], sem.at[s // 8]).start()
    for q in range(src // 8):
        part = pl.ds(q * 8, 8)
        pltpu.make_async_copy(out_v.at[part], out_hbm.at[part], sem.at[q]).wait()


def correlate(active, a, bt):
    parts, wins, src, width = a.shape
    rcv = bt.shape[1]
    return pl.pallas_call(
        correlate_kernel,
        out_shape=jax.ShapeDtypeStruct((src, rcv, LAGS), jnp.float32),
        in_specs=[
            pl.BlockSpec(memory_space=pltpu.SMEM),
            pl.BlockSpec(memory_space=pltpu.VMEM),
            pl.BlockSpec(memory_space=pltpu.VMEM),
        ],
        out_specs=pl.BlockSpec(memory_space=pl.ANY),
        scratch_shapes=[
            pltpu.VMEM((FINE * src, parts * width * wins), jnp.bfloat16),
            pltpu.VMEM((src * LAGS, rcv), jnp.float32),
            pltpu.VMEM((src, rcv, LAGS), jnp.float32),
            pltpu.SemaphoreType.DMA((src // 8,)),
        ],
        compiler_params=pltpu.CompilerParams(vmem_limit_bytes=40 * 2**20),
    )(active, a, bt)


def solution(mesh):
    peers = mesh.shape["rcv"]

    def body(src_traces, rcv_traces, src_owner, rcv_owner, active):
        a, bt = spread(src_owner, rcv_owner, src_traces, rcv_traces, peers)
        return correlate(active, a, bt)

    return jax.shard_map(
        body,
        mesh=mesh,
        in_specs=(
            P(None, "rcv", "src", None),
            P(None, "src", "rcv", None),
            P(None, "src"),
            P(None, "rcv"),
            P("src", "rcv"),
        ),
        out_specs=P("src", "rcv", None),
        check_vma=False,
    )
```

```python
import jax
import jax.numpy as jnp
import numpy as np
from jax import lax
from jax.experimental import pallas as pl
from jax.experimental.pallas import tpu as pltpu
from jax.sharding import PartitionSpec as P

MESH = pl.DeviceIdType.MESH
LAGS = 128
BLOCK = 32
FINE = 16
DEPTH_Z, DEPTH_Y = 8, 4

HOPS = ((0, 1), (0, 1), (1, 1), (2, 0), (0, -1), (0, -1), (-1, -1), (-2, 0))
STREAMS = len(HOPS)
CHUNKS = 8
STEPS = 4
SLACK = 4
A_GATHER = 4
A_ROLL = 12
PASSES = (4, 6, 8)
ROUNDS = CHUNKS + (STEPS - 1) * SLACK
ROUTES = (
    (0, 0, 0, 0, 0, 0, 0, 0, 0, 0, 0, 0, 0, 0, 0, 0, 0, 0, 0, 0, 0, 0, 0, 0),
    (0, 1, 0, 1, 0, 0, 1, 0, 0, 1, 2, 6, 7, 3, 5, 4, 1, 1, 4, 4, 4, 4, 4, 4),
    (6, 1, 0, 1, 2, 3, 0, 1, 0, 1, 7, 6, 4, 5, 3, 2, 2, 2, 3, 3, 2, 2, 3, 3),
    (0, 0, 4, 5, 4, 5, 5, 4, 7, 1, 6, 0, 4, 5, 2, 3, 4, 3, 3, 4, 1, 1, 3, 3),
    (2, 0, 2, 2, 2, 3, 4, 0, 1, 3, 4, 6, 2, 7, 0, 5, 4, 3, 2, 3, 2, 4, 3, 4),
    (3, 2, 2, 2, 2, 3, 0, 2, 4, 6, 2, 7, 0, 5, 1, 3, 3, 4, 1, 3, 3, 4, 4, 3),
    (6, 1, 2, 2, 2, 6, 5, 2, 2, 7, 1, 5, 4, 6, 3, 0, 2, 4, 2, 3, 4, 3, 3, 4),
    (3, 2, 3, 2, 4, 6, 6, 6, 2, 5, 1, 6, 4, 0, 3, 7, 3, 4, 3, 2, 3, 4, 2, 4),
    (2, 3, 3, 3, 2, 7, 3, 0, 1, 4, 6, 3, 5, 0, 2, 7, 4, 3, 3, 1, 4, 3, 3, 3),
    (2, 1, 3, 3, 3, 2, 1, 2, 6, 3, 4, 1, 2, 5, 0, 7, 4, 2, 3, 2, 3, 4, 4, 4),
    (1, 3, 2, 2, 2, 5, 3, 2, 4, 3, 2, 1, 0, 5, 7, 6, 4, 3, 2, 3, 4, 3, 4, 4),
    (3, 2, 3, 3, 2, 3, 3, 2, 2, 1, 6, 0, 7, 3, 4, 5, 3, 4, 4, 4, 4, 2, 4, 4),
    (3, 2, 3, 3, 2, 3, 4, 2, 6, 7, 4, 5, 3, 2, 0, 1, 4, 4, 3, 3, 3, 3, 4, 4),
    (3, 2, 2, 3, 3, 2, 3, 2, 5, 4, 3, 2, 0, 1, 7, 6, 4, 4, 2, 2, 4, 4, 4, 4),
    (1, 2, 3, 3, 2, 3, 3, 2, 3, 2, 0, 1, 7, 6, 5, 4, 3, 3, 3, 3, 4, 4, 4, 4),
    (7, 6, 7, 2, 6, 7, 6, 6, 3, 1, 2, 0, 5, 4, 7, 6, 4, 4, 3, 4, 4, 4, 3, 3),
    (3, 7, 3, 3, 7, 3, 7, 7, 4, 5, 6, 3, 1, 0, 2, 7, 4, 4, 4, 2, 4, 4, 4, 2),
    (3, 7, 3, 0, 7, 3, 7, 1, 7, 3, 5, 0, 2, 6, 4, 1, 3, 3, 4, 3, 4, 4, 4, 3),
    (3, 7, 2, 3, 7, 3, 6, 7, 1, 0, 3, 2, 5, 4, 7, 6, 4, 4, 3, 3, 4, 4, 3, 3),
    (3, 7, 3, 5, 3, 7, 3, 7, 2, 6, 0, 5, 7, 3, 1, 4, 4, 4, 4, 3, 3, 3, 4, 3),
    (0, 7, 7, 6, 7, 6, 7, 7, 6, 7, 4, 5, 3, 2, 1, 0, 3, 3, 4, 4, 4, 4, 3, 3),
    (2, 3, 2, 2, 3, 2, 3, 6, 7, 1, 3, 2, 5, 4, 6, 0, 4, 4, 3, 3, 4, 4, 3, 4),
    (6, 7, 7, 6, 7, 6, 7, 6, 3, 2, 1, 0, 6, 7, 4, 5, 4, 4, 4, 4, 3, 3, 3, 3),
    (6, 7, 7, 6, 7, 6, 6, 7, 5, 4, 3, 2, 0, 1, 7, 6, 4, 4, 4, 4, 4, 4, 2, 2),
    (7, 6, 7, 0, 7, 6, 7, 7, 4, 0, 6, 3, 1, 5, 2, 7, 3, 4, 3, 3, 3, 4, 3, 1),
    (6, 7, 0, 6, 7, 6, 7, 7, 7, 2, 1, 3, 5, 6, 4, 0, 2, 4, 4, 4, 4, 3, 3, 2),
    (6, 1, 4, 6, 6, 4, 6, 6, 1, 7, 3, 2, 4, 0, 6, 5, 3, 3, 4, 4, 3, 4, 2, 3),
    (6, 7, 7, 4, 7, 4, 7, 7, 1, 6, 5, 3, 7, 2, 0, 4, 4, 3, 4, 4, 2, 4, 3, 2),
    (2, 6, 5, 6, 5, 6, 6, 6, 3, 6, 5, 1, 2, 0, 7, 4, 4, 2, 3, 4, 3, 4, 4, 3),
    (1, 7, 2, 2, 2, 7, 7, 6, 6, 1, 7, 3, 0, 5, 4, 2, 3, 3, 2, 4, 4, 3, 3, 2),
    (6, 7, 4, 4, 4, 6, 6, 6, 7, 0, 1, 5, 3, 6, 4, 2, 3, 4, 3, 4, 4, 2, 2, 3),
    (0, 7, 0, 6, 6, 7, 6, 6, 1, 5, 4, 7, 2, 0, 6, 3, 4, 3, 4, 3, 4, 3, 1, 3),
)

epsilon = 1e-06


def normalised(values):
    energy = jnp.mean(values * values, axis=-1, keepdims=True)
    return values * lax.rsqrt(energy + epsilon)


def spread_kernel(
    routes_hbm, src_owner_hbm, rcv_owner_hbm, active_hbm, src_hbm, rcv_hbm,
    lagged,
    routes, src_owner, rcv_owner, active, src_ref, rcv_ref, a_own, a_cand, a_all, own, bt, toep, acc,
    load_sem, send_sem, recv_sem, a_send, a_recv,
    *rest,
):
    wins, _, rcv, samples = rcv_ref.shape
    src = src_ref.shape[2]
    held = [rest[w * ROUNDS : (w + 1) * ROUNDS] for w in range(wins)]
    sent = [rest[(wins + w) * ROUNDS : (wins + w + 1) * ROUNDS] for w in range(wins)]
    place = lax.axis_index("src")
    me = lax.axis_index("rcv")
    z, y = place // DEPTH_Y, place % DEPTH_Y
    others = a_own.shape[0] - 1

    def partner(i):
        dz, dy = HOPS[i]
        return {"src": lax.rem(z + dz + DEPTH_Z, DEPTH_Z) * DEPTH_Y + lax.rem(y + dy + DEPTH_Y, DEPTH_Y)}

    def peer(i):
        return lax.rem(me + 1 + i, others + 1)

    barrier = pltpu.get_barrier_semaphore()
    seen = []
    for i in range(STREAMS):
        if HOPS[i] not in seen:
            seen.append(HOPS[i])
            pl.semaphore_signal(barrier, inc=1, device_id=partner(i), device_id_type=MESH)
    for i in range(others):
        pl.semaphore_signal(barrier, inc=1, device_id={"rcv": peer(i)}, device_id_type=MESH)

    loads = [pltpu.make_async_copy(rcv_hbm.at[w], rcv_ref.at[w], load_sem.at[w]) for w in range(wins)]
    small = ((src_hbm, src_ref), (routes_hbm, routes), (src_owner_hbm, src_owner), (rcv_owner_hbm, rcv_owner), (active_hbm, active))
    loads += [pltpu.make_async_copy(a, b, load_sem.at[wins + i]) for i, (a, b) in enumerate(small)]
    for load in loads:
        load.start()

    width = samples // (others + 1)
    for w in range(wins):
        loads[w].wait()
        rows = normalised(rcv_ref[w, 0].astype(jnp.float32))
        for t in range(samples // LAGS):
            own[pl.ds(w * samples + t * LAGS, LAGS), :] = rows[:, t * LAGS : (t + 1) * LAGS].T.astype(jnp.bfloat16)
    loads[wins].wait()
    for w in range(wins):
        rows = normalised(src_ref[w, 0].astype(jnp.float32)).astype(jnp.bfloat16)
        for i in range(others + 1):
            a_own[i, w] = rows[:, i * width : (i + 1) * width]
    for load in loads[wins + 1 :]:
        load.wait()
    pl.semaphore_wait(barrier, len(seen) + others)

    piece = samples // (CHUNKS * STREAMS)

    def rows_of(w, c, j):
        return pl.ds(w * samples + (c * STREAMS + j) * piece, piece)

    root, row = [], []
    for w in range(wins):
        far = rcv_owner[0, w]
        root.append(far == place)
        dz = lax.rem(z - far // DEPTH_Y + DEPTH_Z, DEPTH_Z)
        dy = lax.rem(y - far % DEPTH_Y + DEPTH_Y, DEPTH_Y)
        row.append((dz * DEPTH_Y + dy) * (3 * STREAMS))

    def arrived(w, r):
        pltpu.make_async_copy(held[w][r], held[w][r], recv_sem.at[w, r]).wait()

    def a_wait(sem, k, ref):
        pltpu.make_async_copy(ref.at[pl.ds(0, others)], ref.at[pl.ds(0, others)], sem.at[k]).wait()

    def a_scatter():
        for i in range(others):
            pltpu.make_async_remote_copy(
                src_ref=a_own.at[peer(i)],
                dst_ref=a_cand.at[me],
                send_sem=a_send.at[0],
                recv_sem=a_recv.at[0],
                device_id={"rcv": peer(i)},
                device_id_type=MESH,
            ).start()

    def a_gather():
        a_wait(a_recv, 0, a_cand)
        for w in range(wins):
            who = src_owner[0, w]
            a_all[me, w] = jnp.where(who == me, a_own[me, w], a_cand[who, w])
        for i in range(others):
            pltpu.make_async_remote_copy(
                src_ref=a_all.at[me],
                dst_ref=a_all.at[me],
                send_sem=a_send.at[1],
                recv_sem=a_recv.at[1],
                device_id={"rcv": peer(i)},
                device_id_type=MESH,
            ).start()

    lane = lax.broadcasted_iota(jnp.int32, (src, samples), 1)

    def roll_part(k):
        for w in range(wins):
            a = jnp.concatenate([a_all[i, w] for i in range(others + 1)], axis=1).astype(jnp.float32)
            a = jnp.where(lane < samples - LAGS, a, 0.0)
            rolled = a if k == 0 else pltpu.roll(a, k, 1)
            toep[pl.ds(k * src, src), w * samples : (w + 1) * samples] = rolled.astype(jnp.bfloat16)

    forward = [[routes[row[w] + i] for i in range(STREAMS)] for w in range(wins)]
    rolled = 0
    for r in range(ROUNDS):
        for w in range(wins):
            if r >= SLACK:
                arrived(w, r - SLACK)
                for i in range(STREAMS):
                    value = held[w][r - SLACK][forward[w][i]]
                    if r < CHUNKS:
                        value = jnp.where(root[w], own[rows_of(w, r, i), :], value)
                    sent[w][r][i] = value
            for i in range(STREAMS):
                pltpu.make_async_remote_copy(
                    src_ref=sent[w][r].at[i] if r >= SLACK else own.at[rows_of(w, min(r, CHUNKS - 1), i), :],
                    dst_ref=held[w][r].at[i],
                    send_sem=send_sem.at[w, r],
                    recv_sem=recv_sem.at[w, r],
                    device_id=partner(i),
                    device_id_type=MESH,
                ).start()
        if r == 0:
            a_scatter()
        if r == A_GATHER:
            a_gather()
        if r == A_ROLL:
            a_wait(a_recv, 1, a_all)
        if r >= A_ROLL:
            upto = FINE * (r - A_ROLL + 1) // (ROUNDS - A_ROLL)
            for k in range(rolled, upto):
                roll_part(k)
            rolled = upto

    slot = [[routes[row[w] + STREAMS + j] for j in range(STREAMS)] for w in range(wins)]
    step = [[routes[row[w] + 2 * STREAMS + j] for j in range(STREAMS)] for w in range(wins)]
    last = (STEPS - 1) * SLACK
    bt[pl.ds(wins * samples, LAGS), :] = jnp.zeros((LAGS, rcv), jnp.bfloat16)
    for r in range(max(0, ROUNDS - SLACK), last):
        for w in range(wins):
            arrived(w, r)
    scale = 1.0 / (float((samples - LAGS) * wins) ** 0.5)
    group = lax.broadcasted_iota(jnp.int32, (1, LAGS), 1) // BLOCK
    factor = jnp.zeros((1, LAGS), jnp.float32)
    for g in range(LAGS // BLOCK):
        factor = jnp.where(group == g, active[0, g].astype(jnp.float32) * scale, factor)

    def product(start, stop, first, final):
        def pair_step(pair, carry):
            base = pl.multiple_of(pair * 2 * FINE, FINE)
            left, right = [], []
            for w in range(wins):
                both = [bt[pl.ds(base + (w * samples + start + FINE * jj), stop - start), :] for jj in range(2)]
                right.append(jnp.concatenate(both, axis=1))
                left.append(toep[:, w * samples + start : w * samples + stop])
            part = jnp.dot(
                jnp.concatenate(left, axis=1), jnp.concatenate(right, axis=0), preferred_element_type=jnp.float32
            )
            columns = pl.ds(pl.multiple_of(pair * 256, 256), 256)
            if not first:
                part = part + acc[:, columns]
            if not final:
                acc[:, columns] = part
            else:
                for jj in range(2):
                    for k in range(FINE):
                        lagged[pl.ds(base + FINE * jj + k, src, stride=LAGS), :] = (
                            part[k * src : (k + 1) * src, jj * LAGS : (jj + 1) * LAGS] * factor
                        )
            return carry

        lax.fori_loop(0, LAGS // FINE // 2, pair_step, 0)

    done = 0
    for c in range(CHUNKS):
        for w in range(wins):
            if c + last >= ROUNDS - SLACK:
                arrived(w, c + last)
            for j in range(STREAMS):
                value = own[rows_of(w, c, j), :]
                for d in range(1, STEPS + 1):
                    value = jnp.where(step[w][j] == d, held[w][c + (d - 1) * SLACK][slot[w][j]], value)
                bt[rows_of(w, c, j), :] = value
        if c + 1 in PASSES:
            stop = samples if c == CHUNKS - 1 else (c + 1) * STREAMS * piece - LAGS
            product(done, stop, done == 0, c == CHUNKS - 1)
            done = stop

    a_wait(a_send, 0, a_all)
    a_wait(a_send, 1, a_all)
    for r in range(ROUNDS):
        for w in range(wins):
            pltpu.make_async_copy(held[w][r], held[w][r], send_sem.at[w, r]).wait()


def spread(src_owner, rcv_owner, active, src_traces, rcv_traces, peers):
    wins, _, src, samples = src_traces.shape
    rcv = rcv_traces.shape[2]
    routes = jnp.asarray(np.array(ROUTES, np.int32).reshape(-1))
    piece = samples // (CHUNKS * STREAMS)
    parts = pltpu.VMEM((peers, wins, src, samples // peers), jnp.bfloat16)
    anywhere = pl.BlockSpec(memory_space=pl.ANY)
    operands = (routes, src_owner.T, rcv_owner.T, active, src_traces, rcv_traces)
    operands = [pltpu.with_memory_space_constraint(v, pltpu.HBM) for v in operands]
    return pl.pallas_call(
        spread_kernel,
        out_shape=jax.ShapeDtypeStruct((src * LAGS, rcv), jnp.float32),
        in_specs=[anywhere] * 6,
        out_specs=pl.BlockSpec(memory_space=pltpu.VMEM),
        scratch_shapes=[
            pltpu.SMEM(routes.shape, jnp.int32),
            pltpu.SMEM((1, wins), jnp.int32),
            pltpu.SMEM((1, wins), jnp.int32),
            pltpu.SMEM(active.shape, jnp.int32),
            pltpu.VMEM(src_traces.shape, jnp.bfloat16),
            pltpu.VMEM(rcv_traces.shape, jnp.bfloat16),
            parts,
            parts,
            parts,
            pltpu.VMEM((wins * samples, rcv), jnp.bfloat16),
            pltpu.VMEM((wins * samples + LAGS, rcv), jnp.bfloat16),
            pltpu.VMEM((FINE * src, wins * samples), jnp.bfloat16),
            pltpu.VMEM((FINE * src, rcv * LAGS // FINE), jnp.float32),
            pltpu.SemaphoreType.DMA((wins + 5,)),
            pltpu.SemaphoreType.DMA((wins, ROUNDS)),
            pltpu.SemaphoreType.DMA((wins, ROUNDS)),
            pltpu.SemaphoreType.DMA((2,)),
            pltpu.SemaphoreType.DMA((2,)),
        ]
        + [pltpu.VMEM((STREAMS, piece, rcv), jnp.bfloat16)] * (2 * wins * ROUNDS),
        compiler_params=pltpu.CompilerParams(collective_id=0, has_side_effects=True, vmem_limit_bytes=48 * 2**20),
    )(*operands)


def finish_kernel(lagged, out_hbm, out_v, sem):
    src = out_v.shape[0]
    for s in range(src):
        out_v[s] = lagged[s * LAGS : (s + 1) * LAGS, :].T
        if s % 4 == 3:
            part = pl.ds(s - 3, 4)
            pltpu.make_async_copy(out_v.at[part], out_hbm.at[part], sem.at[s // 4]).start()
    for q in range(src // 4):
        part = pl.ds(q * 4, 4)
        pltpu.make_async_copy(out_v.at[part], out_hbm.at[part], sem.at[q]).wait()


def finish(lagged):
    rows, rcv = lagged.shape
    src = rows // LAGS
    return pl.pallas_call(
        finish_kernel,
        out_shape=jax.ShapeDtypeStruct((src, rcv, LAGS), jnp.float32),
        in_specs=[pl.BlockSpec(memory_space=pltpu.VMEM)],
        out_specs=pl.BlockSpec(memory_space=pl.ANY),
        scratch_shapes=[pltpu.VMEM((src, rcv, LAGS), jnp.float32), pltpu.SemaphoreType.DMA((src // 4,))],
        compiler_params=pltpu.CompilerParams(vmem_limit_bytes=16 * 2**20),
    )(lagged)


def solution(mesh):
    peers = mesh.shape["rcv"]

    def body(src_traces, rcv_traces, src_owner, rcv_owner, active):
        return finish(spread(src_owner, rcv_owner, active, src_traces, rcv_traces, peers))

    return jax.shard_map(
        body,
        mesh=mesh,
        in_specs=(
            P(None, "rcv", "src", None),
            P(None, "src", "rcv", None),
            P(None, "src"),
            P(None, "rcv"),
            P("src", "rcv"),
        ),
        out_specs=P("src", "rcv", None),
        check_vma=False,
    )
```

```python
import jax
import jax.numpy as jnp
import numpy as np
from jax import lax
from jax.experimental import pallas as pl
from jax.experimental.pallas import tpu as pltpu
from jax.sharding import PartitionSpec as P

MESH = pl.DeviceIdType.MESH
LAGS = 128
BLOCK = 32
FINE = 16
DEPTH_Z, DEPTH_Y = 8, 4

HOPS = ((0, 1), (0, 1), (1, 1), (2, 0), (0, -1), (0, -1), (-1, -1), (-2, 0))
STREAMS = len(HOPS)
CHUNKS = 8
STEPS = 4
SLACK = 4
A_GATHER = 5
A_ROLL = 11
PASSES = (5, 8)
ROUNDS = CHUNKS + (STEPS - 1) * SLACK
ROUTES = (
    (0, 0, 0, 0, 0, 0, 0, 0, 0, 0, 0, 0, 0, 0, 0, 0, 0, 0, 0, 0, 0, 0, 0, 0),
    (0, 1, 0, 1, 0, 0, 1, 0, 0, 1, 2, 6, 7, 3, 5, 4, 1, 1, 4, 4, 4, 4, 4, 4),
    (6, 1, 0, 1, 2, 3, 0, 1, 0, 1, 7, 6, 4, 5, 3, 2, 2, 2, 3, 3, 2, 2, 3, 3),
    (0, 0, 4, 5, 4, 5, 5, 4, 7, 1, 6, 0, 4, 5, 2, 3, 4, 3, 3, 4, 1, 1, 3, 3),
    (2, 0, 2, 2, 2, 3, 4, 0, 1, 3, 4, 6, 2, 7, 0, 5, 4, 3, 2, 3, 2, 4, 3, 4),
    (3, 2, 2, 2, 2, 3, 0, 2, 4, 6, 2, 7, 0, 5, 1, 3, 3, 4, 1, 3, 3, 4, 4, 3),
    (6, 1, 2, 2, 2, 6, 5, 2, 2, 7, 1, 5, 4, 6, 3, 0, 2, 4, 2, 3, 4, 3, 3, 4),
    (3, 2, 3, 2, 4, 6, 6, 6, 2, 5, 1, 6, 4, 0, 3, 7, 3, 4, 3, 2, 3, 4, 2, 4),
    (2, 3, 3, 3, 2, 7, 3, 0, 1, 4, 6, 3, 5, 0, 2, 7, 4, 3, 3, 1, 4, 3, 3, 3),
    (2, 1, 3, 3, 3, 2, 1, 2, 6, 3, 4, 1, 2, 5, 0, 7, 4, 2, 3, 2, 3, 4, 4, 4),
    (1, 3, 2, 2, 2, 5, 3, 2, 4, 3, 2, 1, 0, 5, 7, 6, 4, 3, 2, 3, 4, 3, 4, 4),
    (3, 2, 3, 3, 2, 3, 3, 2, 2, 1, 6, 0, 7, 3, 4, 5, 3, 4, 4, 4, 4, 2, 4, 4),
    (3, 2, 3, 3, 2, 3, 4, 2, 6, 7, 4, 5, 3, 2, 0, 1, 4, 4, 3, 3, 3, 3, 4, 4),
    (3, 2, 2, 3, 3, 2, 3, 2, 5, 4, 3, 2, 0, 1, 7, 6, 4, 4, 2, 2, 4, 4, 4, 4),
    (1, 2, 3, 3, 2, 3, 3, 2, 3, 2, 0, 1, 7, 6, 5, 4, 3, 3, 3, 3, 4, 4, 4, 4),
    (7, 6, 7, 2, 6, 7, 6, 6, 3, 1, 2, 0, 5, 4, 7, 6, 4, 4, 3, 4, 4, 4, 3, 3),
    (3, 7, 3, 3, 7, 3, 7, 7, 4, 5, 6, 3, 1, 0, 2, 7, 4, 4, 4, 2, 4, 4, 4, 2),
    (3, 7, 3, 0, 7, 3, 7, 1, 7, 3, 5, 0, 2, 6, 4, 1, 3, 3, 4, 3, 4, 4, 4, 3),
    (3, 7, 2, 3, 7, 3, 6, 7, 1, 0, 3, 2, 5, 4, 7, 6, 4, 4, 3, 3, 4, 4, 3, 3),
    (3, 7, 3, 5, 3, 7, 3, 7, 2, 6, 0, 5, 7, 3, 1, 4, 4, 4, 4, 3, 3, 3, 4, 3),
    (0, 7, 7, 6, 7, 6, 7, 7, 6, 7, 4, 5, 3, 2, 1, 0, 3, 3, 4, 4, 4, 4, 3, 3),
    (2, 3, 2, 2, 3, 2, 3, 6, 7, 1, 3, 2, 5, 4, 6, 0, 4, 4, 3, 3, 4, 4, 3, 4),
    (6, 7, 7, 6, 7, 6, 7, 6, 3, 2, 1, 0, 6, 7, 4, 5, 4, 4, 4, 4, 3, 3, 3, 3),
    (6, 7, 7, 6, 7, 6, 6, 7, 5, 4, 3, 2, 0, 1, 7, 6, 4, 4, 4, 4, 4, 4, 2, 2),
    (7, 6, 7, 0, 7, 6, 7, 7, 4, 0, 6, 3, 1, 5, 2, 7, 3, 4, 3, 3, 3, 4, 3, 1),
    (6, 7, 0, 6, 7, 6, 7, 7, 7, 2, 1, 3, 5, 6, 4, 0, 2, 4, 4, 4, 4, 3, 3, 2),
    (6, 1, 4, 6, 6, 4, 6, 6, 1, 7, 3, 2, 4, 0, 6, 5, 3, 3, 4, 4, 3, 4, 2, 3),
    (6, 7, 7, 4, 7, 4, 7, 7, 1, 6, 5, 3, 7, 2, 0, 4, 4, 3, 4, 4, 2, 4, 3, 2),
    (2, 6, 5, 6, 5, 6, 6, 6, 3, 6, 5, 1, 2, 0, 7, 4, 4, 2, 3, 4, 3, 4, 4, 3),
    (1, 7, 2, 2, 2, 7, 7, 6, 6, 1, 7, 3, 0, 5, 4, 2, 3, 3, 2, 4, 4, 3, 3, 2),
    (6, 7, 4, 4, 4, 6, 6, 6, 7, 0, 1, 5, 3, 6, 4, 2, 3, 4, 3, 4, 4, 2, 2, 3),
    (0, 7, 0, 6, 6, 7, 6, 6, 1, 5, 4, 7, 2, 0, 6, 3, 4, 3, 4, 3, 4, 3, 1, 3),
)

epsilon = 1e-06


def normalised(values):
    energy = jnp.mean(values * values, axis=-1, keepdims=True)
    return values * lax.rsqrt(energy + epsilon)


def spread_kernel(
    routes_hbm, src_owner_hbm, rcv_owner_hbm, active_hbm, src_hbm, rcv_hbm,
    lagged,
    routes, src_owner, rcv_owner, active, src_ref, rcv_ref, a_own, a_cand, a_all, own, bt, toep, acc,
    load_sem, send_sem, recv_sem, a_send, a_recv,
    *rest,
):
    wins, _, rcv, samples = rcv_ref.shape
    src = src_ref.shape[2]
    held = [rest[w * ROUNDS : (w + 1) * ROUNDS] for w in range(wins)]
    sent = [rest[(wins + w) * ROUNDS : (wins + w + 1) * ROUNDS] for w in range(wins)]
    place = lax.axis_index("src")
    me = lax.axis_index("rcv")
    z, y = place // DEPTH_Y, place % DEPTH_Y
    others = a_own.shape[0] - 1

    def partner(i):
        dz, dy = HOPS[i]
        return {"src": lax.rem(z + dz + DEPTH_Z, DEPTH_Z) * DEPTH_Y + lax.rem(y + dy + DEPTH_Y, DEPTH_Y)}

    def peer(i):
        return lax.rem(me + 1 + i, others + 1)

    barrier = pltpu.get_barrier_semaphore()
    seen = []
    for i in range(STREAMS):
        if HOPS[i] not in seen:
            seen.append(HOPS[i])
            pl.semaphore_signal(barrier, inc=1, device_id=partner(i), device_id_type=MESH)
    for i in range(others):
        pl.semaphore_signal(barrier, inc=1, device_id={"rcv": peer(i)}, device_id_type=MESH)

    loads = [pltpu.make_async_copy(rcv_hbm.at[w], rcv_ref.at[w], load_sem.at[w]) for w in range(wins)]
    small = ((src_hbm, src_ref), (routes_hbm, routes), (src_owner_hbm, src_owner), (rcv_owner_hbm, rcv_owner), (active_hbm, active))
    loads += [pltpu.make_async_copy(a, b, load_sem.at[wins + i]) for i, (a, b) in enumerate(small)]
    for load in loads:
        load.start()

    width = samples // (others + 1)

    def ready_receivers(w):
        loads[w].wait()
        rows = normalised(rcv_ref[w, 0].astype(jnp.float32))
        for t in range(samples // LAGS):
            own[pl.ds(w * samples + t * LAGS, LAGS), :] = rows[:, t * LAGS : (t + 1) * LAGS].T.astype(jnp.bfloat16)

    def ready_sources():
        loads[wins].wait()
        for w in range(wins):
            rows = normalised(src_ref[w, 0].astype(jnp.float32)).astype(jnp.bfloat16)
            for i in range(others + 1):
                a_own[i, w] = rows[:, i * width : (i + 1) * width]

    ready_receivers(0)
    for load in loads[wins + 1 :]:
        load.wait()
    pl.semaphore_wait(barrier, len(seen) + others)

    piece = samples // (CHUNKS * STREAMS)

    def rows_of(w, c, j):
        return pl.ds(w * samples + (c * STREAMS + j) * piece, piece)

    root, row = [], []
    for w in range(wins):
        far = rcv_owner[0, w]
        root.append(far == place)
        dz = lax.rem(z - far // DEPTH_Y + DEPTH_Z, DEPTH_Z)
        dy = lax.rem(y - far % DEPTH_Y + DEPTH_Y, DEPTH_Y)
        row.append((dz * DEPTH_Y + dy) * (3 * STREAMS))

    def arrived(w, r):
        pltpu.make_async_copy(held[w][r], held[w][r], recv_sem.at[w, r]).wait()

    def a_wait(sem, k, ref):
        pltpu.make_async_copy(ref.at[pl.ds(0, others)], ref.at[pl.ds(0, others)], sem.at[k]).wait()

    def a_scatter():
        for i in range(others):
            pltpu.make_async_remote_copy(
                src_ref=a_own.at[peer(i)],
                dst_ref=a_cand.at[me],
                send_sem=a_send.at[0],
                recv_sem=a_recv.at[0],
                device_id={"rcv": peer(i)},
                device_id_type=MESH,
            ).start()

    def a_gather():
        a_wait(a_recv, 0, a_cand)
        for w in range(wins):
            who = src_owner[0, w]
            a_all[me, w] = jnp.where(who == me, a_own[me, w], a_cand[who, w])
        for i in range(others):
            pltpu.make_async_remote_copy(
                src_ref=a_all.at[me],
                dst_ref=a_all.at[me],
                send_sem=a_send.at[1],
                recv_sem=a_recv.at[1],
                device_id={"rcv": peer(i)},
                device_id_type=MESH,
            ).start()

    lane = lax.broadcasted_iota(jnp.int32, (src, samples), 1)

    def roll_part(k):
        for w in range(wins):
            a = jnp.concatenate([a_all[i, w] for i in range(others + 1)], axis=1).astype(jnp.float32)
            a = jnp.where(lane < samples - LAGS, a, 0.0)
            rolled = a if k == 0 else pltpu.roll(a, k, 1)
            toep[pl.ds(k * src, src), w * samples : (w + 1) * samples] = rolled.astype(jnp.bfloat16)

    forward = [[routes[row[w] + i] for i in range(STREAMS)] for w in range(wins)]
    rolled = 0
    for r in range(ROUNDS):
        for w in range(wins):
            if r == 0 and w > 0:
                ready_receivers(w)
            if r >= SLACK:
                arrived(w, r - SLACK)
                for i in range(STREAMS):
                    value = held[w][r - SLACK][forward[w][i]]
                    if r < CHUNKS:
                        value = jnp.where(root[w], own[rows_of(w, r, i), :], value)
                    sent[w][r][i] = value
            for i in range(STREAMS):
                pltpu.make_async_remote_copy(
                    src_ref=sent[w][r].at[i] if r >= SLACK else own.at[rows_of(w, min(r, CHUNKS - 1), i), :],
                    dst_ref=held[w][r].at[i],
                    send_sem=send_sem.at[w, r],
                    recv_sem=recv_sem.at[w, r],
                    device_id=partner(i),
                    device_id_type=MESH,
                ).start()
        if r == 1:
            ready_sources()
            a_scatter()
        if r == A_GATHER:
            a_gather()
        if r == A_ROLL:
            a_wait(a_recv, 1, a_all)
        if r >= A_ROLL:
            upto = FINE * (r - A_ROLL + 1) // (ROUNDS - A_ROLL)
            for k in range(rolled, upto):
                roll_part(k)
            rolled = upto

    slot = [[routes[row[w] + STREAMS + j] for j in range(STREAMS)] for w in range(wins)]
    step = [[routes[row[w] + 2 * STREAMS + j] for j in range(STREAMS)] for w in range(wins)]
    last = (STEPS - 1) * SLACK
    bt[pl.ds(wins * samples, LAGS), :] = jnp.zeros((LAGS, rcv), jnp.bfloat16)
    for r in range(max(0, ROUNDS - SLACK), last):
        for w in range(wins):
            arrived(w, r)
    scale = 1.0 / (float((samples - LAGS) * wins) ** 0.5)
    group = lax.broadcasted_iota(jnp.int32, (1, LAGS), 1) // BLOCK
    factor = jnp.zeros((1, LAGS), jnp.float32)
    for g in range(LAGS // BLOCK):
        factor = jnp.where(group == g, active[0, g].astype(jnp.float32) * scale, factor)

    def product(start, stop, first, final):
        def pair_step(pair, carry):
            base = pl.multiple_of(pair * 2 * FINE, FINE)
            left, right = [], []
            for w in range(wins):
                both = [bt[pl.ds(base + (w * samples + start + FINE * jj), stop - start), :] for jj in range(2)]
                right.append(jnp.concatenate(both, axis=1))
                left.append(toep[:, w * samples + start : w * samples + stop])
            part = jnp.dot(
                jnp.concatenate(left, axis=1), jnp.concatenate(right, axis=0), preferred_element_type=jnp.float32
            )
            columns = pl.ds(pl.multiple_of(pair * 256, 256), 256)
            if not first:
                part = part + acc[:, columns]
            if not final:
                acc[:, columns] = part
            else:
                for jj in range(2):
                    for k in range(FINE):
                        lagged[pl.ds(base + FINE * jj + k, src, stride=LAGS), :] = (
                            part[k * src : (k + 1) * src, jj * LAGS : (jj + 1) * LAGS] * factor
                        )
            return carry

        lax.fori_loop(0, LAGS // FINE // 2, pair_step, 0)

    done = 0
    for c in range(CHUNKS):
        for w in range(wins):
            if c + last >= ROUNDS - SLACK:
                arrived(w, c + last)
            for j in range(STREAMS):
                value = own[rows_of(w, c, j), :]
                for d in range(1, STEPS + 1):
                    value = jnp.where(step[w][j] == d, held[w][c + (d - 1) * SLACK][slot[w][j]], value)
                bt[rows_of(w, c, j), :] = value
        if c + 1 in PASSES:
            stop = samples if c == CHUNKS - 1 else (c + 1) * STREAMS * piece - LAGS
            product(done, stop, done == 0, c == CHUNKS - 1)
            done = stop

    a_wait(a_send, 0, a_all)
    a_wait(a_send, 1, a_all)
    for r in range(ROUNDS):
        for w in range(wins):
            pltpu.make_async_copy(held[w][r], held[w][r], send_sem.at[w, r]).wait()


def spread(src_owner, rcv_owner, active, src_traces, rcv_traces, peers):
    wins, _, src, samples = src_traces.shape
    rcv = rcv_traces.shape[2]
    routes = jnp.asarray(np.array(ROUTES, np.int32).reshape(-1))
    piece = samples // (CHUNKS * STREAMS)
    parts = pltpu.VMEM((peers, wins, src, samples // peers), jnp.bfloat16)
    anywhere = pl.BlockSpec(memory_space=pl.ANY)
    operands = (routes, src_owner.T, rcv_owner.T, active, src_traces, rcv_traces)
    operands = [pltpu.with_memory_space_constraint(v, pltpu.HBM) for v in operands]
    return pl.pallas_call(
        spread_kernel,
        out_shape=jax.ShapeDtypeStruct((src * LAGS, rcv), jnp.float32),
        in_specs=[anywhere] * 6,
        out_specs=pl.BlockSpec(memory_space=pltpu.VMEM),
        scratch_shapes=[
            pltpu.SMEM(routes.shape, jnp.int32),
            pltpu.SMEM((1, wins), jnp.int32),
            pltpu.SMEM((1, wins), jnp.int32),
            pltpu.SMEM(active.shape, jnp.int32),
            pltpu.VMEM(src_traces.shape, jnp.bfloat16),
            pltpu.VMEM(rcv_traces.shape, jnp.bfloat16),
            parts,
            parts,
            parts,
            pltpu.VMEM((wins * samples, rcv), jnp.bfloat16),
            pltpu.VMEM((wins * samples + LAGS, rcv), jnp.bfloat16),
            pltpu.VMEM((FINE * src, wins * samples), jnp.bfloat16),
            pltpu.VMEM((FINE * src, rcv * LAGS // FINE), jnp.float32),
            pltpu.SemaphoreType.DMA((wins + 5,)),
            pltpu.SemaphoreType.DMA((wins, ROUNDS)),
            pltpu.SemaphoreType.DMA((wins, ROUNDS)),
            pltpu.SemaphoreType.DMA((2,)),
            pltpu.SemaphoreType.DMA((2,)),
        ]
        + [pltpu.VMEM((STREAMS, piece, rcv), jnp.bfloat16)] * (2 * wins * ROUNDS),
        compiler_params=pltpu.CompilerParams(collective_id=0, has_side_effects=True, vmem_limit_bytes=48 * 2**20),
    )(*operands)


def finish_kernel(lagged, out_hbm, out_v, sem):
    src = out_v.shape[0]
    for s in range(src):
        out_v[s] = lagged[s * LAGS : (s + 1) * LAGS, :].T
        if s % 4 == 3:
            part = pl.ds(s - 3, 4)
            pltpu.make_async_copy(out_v.at[part], out_hbm.at[part], sem.at[s // 4]).start()
    for q in range(src // 4):
        part = pl.ds(q * 4, 4)
        pltpu.make_async_copy(out_v.at[part], out_hbm.at[part], sem.at[q]).wait()


def finish(lagged):
    rows, rcv = lagged.shape
    src = rows // LAGS
    return pl.pallas_call(
        finish_kernel,
        out_shape=jax.ShapeDtypeStruct((src, rcv, LAGS), jnp.float32),
        in_specs=[pl.BlockSpec(memory_space=pltpu.VMEM)],
        out_specs=pl.BlockSpec(memory_space=pl.ANY),
        scratch_shapes=[pltpu.VMEM((src, rcv, LAGS), jnp.float32), pltpu.SemaphoreType.DMA((src // 4,))],
        compiler_params=pltpu.CompilerParams(vmem_limit_bytes=16 * 2**20),
    )(lagged)


def solution(mesh):
    peers = mesh.shape["rcv"]

    def body(src_traces, rcv_traces, src_owner, rcv_owner, active):
        return finish(spread(src_owner, rcv_owner, active, src_traces, rcv_traces, peers))

    return jax.shard_map(
        body,
        mesh=mesh,
        in_specs=(
            P(None, "rcv", "src", None),
            P(None, "src", "rcv", None),
            P(None, "src"),
            P(None, "rcv"),
            P("src", "rcv"),
        ),
        out_specs=P("src", "rcv", None),
        check_vma=False,
    )
```

```python
import functools

import jax
import jax.numpy as jnp
import numpy as np
from jax import lax
from jax.experimental import pallas as pl
from jax.experimental.pallas import tpu as pltpu
from jax.sharding import PartitionSpec as P

MESH = pl.DeviceIdType.MESH
LAGS = 128
BLOCK = 32
FINE = 16
DEPTH_Z, DEPTH_Y = 8, 4

HOPS = ((0, 1), (0, 1), (1, 1), (2, 0), (0, -1), (0, -1), (-1, -1), (-2, 0))
STREAMS = len(HOPS)
CHUNKS = 8
STEPS = 4
SLACK = 4
A_GATHER = 5
A_ROLL = 11
PASSES = (4, 8)
ROUNDS = CHUNKS + (STEPS - 1) * SLACK
ROUTES = (
    (0, 0, 0, 0, 0, 0, 0, 0, 0, 0, 0, 0, 0, 0, 0, 0, 0, 0, 0, 0, 0, 0, 0, 0),
    (0, 1, 0, 1, 0, 0, 1, 0, 0, 1, 2, 6, 7, 3, 5, 4, 1, 1, 4, 4, 4, 4, 4, 4),
    (6, 1, 0, 1, 2, 3, 0, 1, 0, 1, 7, 6, 4, 5, 3, 2, 2, 2, 3, 3, 2, 2, 3, 3),
    (0, 0, 4, 5, 4, 5, 5, 4, 7, 1, 6, 0, 4, 5, 2, 3, 4, 3, 3, 4, 1, 1, 3, 3),
    (2, 0, 2, 2, 2, 3, 4, 0, 1, 3, 4, 6, 2, 7, 0, 5, 4, 3, 2, 3, 2, 4, 3, 4),
    (3, 2, 2, 2, 2, 3, 0, 2, 4, 6, 2, 7, 0, 5, 1, 3, 3, 4, 1, 3, 3, 4, 4, 3),
    (6, 1, 2, 2, 2, 6, 5, 2, 2, 7, 1, 5, 4, 6, 3, 0, 2, 4, 2, 3, 4, 3, 3, 4),
    (3, 2, 3, 2, 4, 6, 6, 6, 2, 5, 1, 6, 4, 0, 3, 7, 3, 4, 3, 2, 3, 4, 2, 4),
    (2, 3, 3, 3, 2, 7, 3, 0, 1, 4, 6, 3, 5, 0, 2, 7, 4, 3, 3, 1, 4, 3, 3, 3),
    (2, 1, 3, 3, 3, 2, 1, 2, 6, 3, 4, 1, 2, 5, 0, 7, 4, 2, 3, 2, 3, 4, 4, 4),
    (1, 3, 2, 2, 2, 5, 3, 2, 4, 3, 2, 1, 0, 5, 7, 6, 4, 3, 2, 3, 4, 3, 4, 4),
    (3, 2, 3, 3, 2, 3, 3, 2, 2, 1, 6, 0, 7, 3, 4, 5, 3, 4, 4, 4, 4, 2, 4, 4),
    (3, 2, 3, 3, 2, 3, 4, 2, 6, 7, 4, 5, 3, 2, 0, 1, 4, 4, 3, 3, 3, 3, 4, 4),
    (3, 2, 2, 3, 3, 2, 3, 2, 5, 4, 3, 2, 0, 1, 7, 6, 4, 4, 2, 2, 4, 4, 4, 4),
    (1, 2, 3, 3, 2, 3, 3, 2, 3, 2, 0, 1, 7, 6, 5, 4, 3, 3, 3, 3, 4, 4, 4, 4),
    (7, 6, 7, 2, 6, 7, 6, 6, 3, 1, 2, 0, 5, 4, 7, 6, 4, 4, 3, 4, 4, 4, 3, 3),
    (3, 7, 3, 3, 7, 3, 7, 7, 4, 5, 6, 3, 1, 0, 2, 7, 4, 4, 4, 2, 4, 4, 4, 2),
    (3, 7, 3, 0, 7, 3, 7, 1, 7, 3, 5, 0, 2, 6, 4, 1, 3, 3, 4, 3, 4, 4, 4, 3),
    (3, 7, 2, 3, 7, 3, 6, 7, 1, 0, 3, 2, 5, 4, 7, 6, 4, 4, 3, 3, 4, 4, 3, 3),
    (3, 7, 3, 5, 3, 7, 3, 7, 2, 6, 0, 5, 7, 3, 1, 4, 4, 4, 4, 3, 3, 3, 4, 3),
    (0, 7, 7, 6, 7, 6, 7, 7, 6, 7, 4, 5, 3, 2, 1, 0, 3, 3, 4, 4, 4, 4, 3, 3),
    (2, 3, 2, 2, 3, 2, 3, 6, 7, 1, 3, 2, 5, 4, 6, 0, 4, 4, 3, 3, 4, 4, 3, 4),
    (6, 7, 7, 6, 7, 6, 7, 6, 3, 2, 1, 0, 6, 7, 4, 5, 4, 4, 4, 4, 3, 3, 3, 3),
    (6, 7, 7, 6, 7, 6, 6, 7, 5, 4, 3, 2, 0, 1, 7, 6, 4, 4, 4, 4, 4, 4, 2, 2),
    (7, 6, 7, 0, 7, 6, 7, 7, 4, 0, 6, 3, 1, 5, 2, 7, 3, 4, 3, 3, 3, 4, 3, 1),
    (6, 7, 0, 6, 7, 6, 7, 7, 7, 2, 1, 3, 5, 6, 4, 0, 2, 4, 4, 4, 4, 3, 3, 2),
    (6, 1, 4, 6, 6, 4, 6, 6, 1, 7, 3, 2, 4, 0, 6, 5, 3, 3, 4, 4, 3, 4, 2, 3),
    (6, 7, 7, 4, 7, 4, 7, 7, 1, 6, 5, 3, 7, 2, 0, 4, 4, 3, 4, 4, 2, 4, 3, 2),
    (2, 6, 5, 6, 5, 6, 6, 6, 3, 6, 5, 1, 2, 0, 7, 4, 4, 2, 3, 4, 3, 4, 4, 3),
    (1, 7, 2, 2, 2, 7, 7, 6, 6, 1, 7, 3, 0, 5, 4, 2, 3, 3, 2, 4, 4, 3, 3, 2),
    (6, 7, 4, 4, 4, 6, 6, 6, 7, 0, 1, 5, 3, 6, 4, 2, 3, 4, 3, 4, 4, 2, 2, 3),
    (0, 7, 0, 6, 6, 7, 6, 6, 1, 5, 4, 7, 2, 0, 6, 3, 4, 3, 4, 3, 4, 3, 1, 3),
)

epsilon = 1e-06


def normalised(values):
    energy = jnp.mean(values * values, axis=-1, keepdims=True)
    return values * lax.rsqrt(energy + epsilon)


def spread_kernel(
    routes_hbm, src_owner_hbm, rcv_owner_hbm, active_hbm, src_hbm, rcv_hbm,
    acc,
    routes, src_owner, rcv_owner, active, src_ref, rcv_ref, a_own, a_cand, a_all, own, bt, toep,
    load_sem, send_sem, recv_sem, a_send, a_recv,
    *rest,
):
    wins, _, rcv, samples = rcv_ref.shape
    src = src_ref.shape[2]
    held = [rest[w * ROUNDS : (w + 1) * ROUNDS] for w in range(wins)]
    sent = [rest[(wins + w) * ROUNDS : (wins + w + 1) * ROUNDS] for w in range(wins)]
    place = lax.axis_index("src")
    me = lax.axis_index("rcv")
    z, y = place // DEPTH_Y, place % DEPTH_Y
    others = a_own.shape[0] - 1

    def partner(i):
        dz, dy = HOPS[i]
        return {"src": lax.rem(z + dz + DEPTH_Z, DEPTH_Z) * DEPTH_Y + lax.rem(y + dy + DEPTH_Y, DEPTH_Y)}

    def peer(i):
        return lax.rem(me + 1 + i, others + 1)

    barrier = pltpu.get_barrier_semaphore()
    seen = []
    for i in range(STREAMS):
        if HOPS[i] not in seen:
            seen.append(HOPS[i])
            pl.semaphore_signal(barrier, inc=1, device_id=partner(i), device_id_type=MESH)
    for i in range(others):
        pl.semaphore_signal(barrier, inc=1, device_id={"rcv": peer(i)}, device_id_type=MESH)

    loads = [pltpu.make_async_copy(rcv_hbm.at[w], rcv_ref.at[w], load_sem.at[w]) for w in range(wins)]
    small = ((src_hbm, src_ref), (routes_hbm, routes), (src_owner_hbm, src_owner), (rcv_owner_hbm, rcv_owner), (active_hbm, active))
    loads += [pltpu.make_async_copy(a, b, load_sem.at[wins + i]) for i, (a, b) in enumerate(small)]
    for load in loads:
        load.start()

    width = samples // (others + 1)

    def ready_receivers(w):
        loads[w].wait()
        rows = normalised(rcv_ref[w, 0].astype(jnp.float32))
        for t in range(samples // LAGS):
            own[pl.ds(w * samples + t * LAGS, LAGS), :] = rows[:, t * LAGS : (t + 1) * LAGS].T.astype(jnp.bfloat16)

    def ready_sources():
        loads[wins].wait()
        for w in range(wins):
            rows = normalised(src_ref[w, 0].astype(jnp.float32)).astype(jnp.bfloat16)
            for i in range(others + 1):
                a_own[i, w] = rows[:, i * width : (i + 1) * width]

    ready_receivers(0)
    for load in loads[wins + 1 :]:
        load.wait()
    pl.semaphore_wait(barrier, len(seen) + others)

    piece = samples // (CHUNKS * STREAMS)

    def rows_of(w, c, j):
        return pl.ds(w * samples + (c * STREAMS + j) * piece, piece)

    root, row = [], []
    for w in range(wins):
        far = rcv_owner[0, w]
        root.append(far == place)
        dz = lax.rem(z - far // DEPTH_Y + DEPTH_Z, DEPTH_Z)
        dy = lax.rem(y - far % DEPTH_Y + DEPTH_Y, DEPTH_Y)
        row.append((dz * DEPTH_Y + dy) * (3 * STREAMS))

    def arrived(w, r):
        pltpu.make_async_copy(held[w][r], held[w][r], recv_sem.at[w, r]).wait()

    def a_wait(sem, k, ref):
        pltpu.make_async_copy(ref.at[pl.ds(0, others)], ref.at[pl.ds(0, others)], sem.at[k]).wait()

    def a_scatter():
        for i in range(others):
            pltpu.make_async_remote_copy(
                src_ref=a_own.at[peer(i)],
                dst_ref=a_cand.at[me],
                send_sem=a_send.at[0],
                recv_sem=a_recv.at[0],
                device_id={"rcv": peer(i)},
                device_id_type=MESH,
            ).start()

    def a_gather():
        a_wait(a_recv, 0, a_cand)
        for w in range(wins):
            who = src_owner[0, w]
            a_all[me, w] = jnp.where(who == me, a_own[me, w], a_cand[who, w])
        for i in range(others):
            pltpu.make_async_remote_copy(
                src_ref=a_all.at[me],
                dst_ref=a_all.at[me],
                send_sem=a_send.at[1],
                recv_sem=a_recv.at[1],
                device_id={"rcv": peer(i)},
                device_id_type=MESH,
            ).start()

    lane = lax.broadcasted_iota(jnp.int32, (src, samples), 1)

    def roll_part(k):
        for w in range(wins):
            a = jnp.concatenate([a_all[i, w] for i in range(others + 1)], axis=1).astype(jnp.float32)
            a = jnp.where(lane < samples - LAGS, a, 0.0)
            rolled = pltpu.roll(a, LAGS - FINE + k, 1)
            toep[pl.ds(k * src, src), w * samples : (w + 1) * samples] = rolled.astype(jnp.bfloat16)

    slot = [[routes[row[w] + STREAMS + j] for j in range(STREAMS)] for w in range(wins)]
    step = [[routes[row[w] + 2 * STREAMS + j] for j in range(STREAMS)] for w in range(wins)]
    last = (STEPS - 1) * SLACK

    deep = LAGS + samples
    group = lax.broadcasted_iota(jnp.int32, (1, rcv), 1) // BLOCK
    listed = jnp.zeros((1, rcv), jnp.float32)
    for g in range(rcv // BLOCK):
        listed = jnp.where(group == g, active[0, g].astype(jnp.float32), listed)
    listed = listed.astype(jnp.bfloat16)

    def gather_chunk(c):
        for w in range(wins):
            for j in range(STREAMS):
                value = own[rows_of(w, c, j), :]
                for d in range(1, STEPS + 1):
                    value = jnp.where(step[w][j] == d, held[w][c + (d - 1) * SLACK][slot[w][j]], value)
                bt[pl.ds(w * deep + LAGS + (c * STREAMS + j) * piece, piece), :] = value * listed

    forward = [[routes[row[w] + i] for i in range(STREAMS)] for w in range(wins)]
    rolled = 0
    for r in range(ROUNDS):
        for w in range(wins):
            if r == 0 and w > 0:
                ready_receivers(w)
            if r >= SLACK:
                arrived(w, r - SLACK)
                for i in range(STREAMS):
                    value = held[w][r - SLACK][forward[w][i]]
                    if r < CHUNKS:
                        value = jnp.where(root[w], own[rows_of(w, r, i), :], value)
                    sent[w][r][i] = value
            for i in range(STREAMS):
                pltpu.make_async_remote_copy(
                    src_ref=sent[w][r].at[i] if r >= SLACK else own.at[rows_of(w, min(r, CHUNKS - 1), i), :],
                    dst_ref=held[w][r].at[i],
                    send_sem=send_sem.at[w, r],
                    recv_sem=recv_sem.at[w, r],
                    device_id=partner(i),
                    device_id_type=MESH,
                ).start()
        if r == 2:
            acc[...] = jnp.zeros_like(acc)
            for w in range(wins):
                bt[pl.ds(w * deep, LAGS), :] = jnp.zeros((LAGS, rcv), jnp.bfloat16)
        if r == 1:
            ready_sources()
            a_scatter()
        if r == A_GATHER:
            a_gather()
        if r == A_ROLL:
            a_wait(a_recv, 1, a_all)
        if r >= A_ROLL:
            upto = FINE * (r - A_ROLL + 1) // (ROUNDS - A_ROLL)
            for k in range(rolled, upto):
                roll_part(k)
            rolled = upto
        if r - SLACK >= last:
            gather_chunk(r - SLACK - last)

    half = samples // 2

    def part_step(at, carry):
        late, pair = at // 4, at % 4

        @pl.when(at == 4)
        def _():
            for c in range(CHUNKS - SLACK, CHUNKS):
                for w in range(wins):
                    arrived(w, c + last)
                gather_chunk(c)
            a_wait(a_send, 0, a_all)
            a_wait(a_send, 1, a_all)
            for r in range(ROUNDS):
                for w in range(wins):
                    pltpu.make_async_copy(held[w][r], held[w][r], send_sem.at[w, r]).wait()

        start = pl.multiple_of(late * half, half)
        base = pl.multiple_of(late * half + pair * 2 * FINE, FINE)
        left, right = [], []
        for w in range(wins):
            both = [bt[pl.ds(base + (w * deep + FINE + FINE * jj), half), :] for jj in range(2)]
            right.append(jnp.concatenate(both, axis=1))
            left.append(toep[:, pl.ds(pl.multiple_of(w * samples + start, half), half)])
        part = jnp.dot(
            jnp.concatenate(left, axis=1), jnp.concatenate(right, axis=0), preferred_element_type=jnp.float32
        )
        for jj in range(2):
            acc[2 * pair + jj] += part[:, jj * rcv : (jj + 1) * rcv]
        return carry

    lax.fori_loop(0, 8, part_step, 0)


def spread(src_owner, rcv_owner, active, src_traces, rcv_traces, peers):
    wins, _, src, samples = src_traces.shape
    rcv = rcv_traces.shape[2]
    routes = jnp.asarray(np.array(ROUTES, np.int32).reshape(-1))
    piece = samples // (CHUNKS * STREAMS)
    parts = pltpu.VMEM((peers, wins, src, samples // peers), jnp.bfloat16)
    anywhere = pl.BlockSpec(memory_space=pl.ANY)
    operands = (routes, src_owner.T, rcv_owner.T, active, src_traces, rcv_traces)
    operands = [pltpu.with_memory_space_constraint(v, pltpu.HBM) for v in operands]
    return pl.pallas_call(
        spread_kernel,
        out_shape=jax.ShapeDtypeStruct((LAGS // FINE, FINE * src, rcv), jnp.float32),
        in_specs=[anywhere] * 6,
        out_specs=pl.BlockSpec(memory_space=pltpu.VMEM),
        scratch_shapes=[
            pltpu.SMEM(routes.shape, jnp.int32),
            pltpu.SMEM((1, wins), jnp.int32),
            pltpu.SMEM((1, wins), jnp.int32),
            pltpu.SMEM(active.shape, jnp.int32),
            pltpu.VMEM(src_traces.shape, jnp.bfloat16),
            pltpu.VMEM(rcv_traces.shape, jnp.bfloat16),
            parts,
            parts,
            parts,
            pltpu.VMEM((wins * samples, rcv), jnp.bfloat16),
            pltpu.VMEM((wins * (samples + LAGS), rcv), jnp.bfloat16),
            pltpu.VMEM((FINE * src, wins * samples), jnp.bfloat16),
            pltpu.SemaphoreType.DMA((wins + 5,)),
            pltpu.SemaphoreType.DMA((wins, ROUNDS)),
            pltpu.SemaphoreType.DMA((wins, ROUNDS)),
            pltpu.SemaphoreType.DMA((2,)),
            pltpu.SemaphoreType.DMA((2,)),
        ]
        + [pltpu.VMEM((STREAMS, piece, rcv), jnp.bfloat16)] * (2 * wins * ROUNDS),
        compiler_params=pltpu.CompilerParams(collective_id=0, has_side_effects=True, vmem_limit_bytes=48 * 2**20),
    )(*operands)


def finish_kernel(scale, acc, out_hbm, out_v, sem):
    src = out_v.shape[0]
    for s in range(src):
        lags = [acc[j, pl.ds(s, FINE, stride=src), :] for j in range(LAGS // FINE)]
        out_v[s] = (jnp.concatenate(lags, axis=0) * scale).T
        if s % 4 == 3:
            part = pl.ds(s - 3, 4)
            pltpu.make_async_copy(out_v.at[part], out_hbm.at[part], sem.at[s // 4]).start()
    for q in range(src // 4):
        part = pl.ds(q * 4, 4)
        pltpu.make_async_copy(out_v.at[part], out_hbm.at[part], sem.at[q]).wait()


def finish(acc, scale):
    _, rows, rcv = acc.shape
    src = rows // FINE
    return pl.pallas_call(
        functools.partial(finish_kernel, scale),
        out_shape=jax.ShapeDtypeStruct((src, rcv, LAGS), jnp.float32),
        in_specs=[pl.BlockSpec(memory_space=pltpu.VMEM)],
        out_specs=pl.BlockSpec(memory_space=pl.ANY),
        scratch_shapes=[pltpu.VMEM((src, rcv, LAGS), jnp.float32), pltpu.SemaphoreType.DMA((src // 4,))],
        compiler_params=pltpu.CompilerParams(vmem_limit_bytes=16 * 2**20),
    )(acc)


def solution(mesh):
    peers = mesh.shape["rcv"]

    def body(src_traces, rcv_traces, src_owner, rcv_owner, active):
        wins, _, _, samples = src_traces.shape
        scale = 1.0 / (float((samples - LAGS) * wins) ** 0.5)
        return finish(spread(src_owner, rcv_owner, active, src_traces, rcv_traces, peers), scale)

    return jax.shard_map(
        body,
        mesh=mesh,
        in_specs=(
            P(None, "rcv", "src", None),
            P(None, "src", "rcv", None),
            P(None, "src"),
            P(None, "rcv"),
            P("src", "rcv"),
        ),
        out_specs=P("src", "rcv", None),
        check_vma=False,
    )
```
